512 devices in a mesh: rx: 16 (over z_hi, x, core), ry: 4 (over y), tp: 8 (over z_lo).
Axes of the slice: x: 4, y: 4, z: 16 (z_hi: 2, z_lo: 8; z = z_hi * 8 + z_lo), core: 2. Of those that a mesh axis runs over, the one named last changes fastest.
Arguments:
- weights: bfloat16 [16, 4, 3, 160, 4096], P('rx', 'ry', None, 'tp'), may hold values from -6 to 6
- tracker: bfloat16 [16, 4, 3, 160, 4096], P('rx', 'ry', None, 'tp'), may hold values from -6 to 6
- acts: bfloat16 [16, 4, 1024, 4096], P('rx', 'ry', 'tp'), may hold values from -6 to 6
- cotangent: bfloat16 [16, 4, 1024, 4096], P('rx', 'ry', 'tp'), may hold values from -6 to 6
Outputs:
- new_weights: bfloat16 [16, 4, 3, 160, 4096], P('rx', 'ry', None, 'tp')
- new_tracker: bfloat16 [16, 4, 3, 160, 4096], P('rx', 'ry', None, 'tp')
The draws below stay inside these ranges and needn't reach their ends.
All inputs are finite; a program needn't handle non-finite values.
Results may differ from the reference program's by a relative error of at most 0.019.
Values may be sent and summed in bfloat16 or wider, within the bound.
A program may use at most 128 MiB of HBM per device.

```python
import jax
import jax.numpy as jnp
from jax import lax

D = 4096
TOK_DEV = 128
SLAB = 160
TOKENS = 1024
N_RX = 16
N_RY = 4
N_TP = 8


def block_levels(key, shape, shards, least, top_value):
    factor_of, own = 1.0, jax.random.fold_in(key, 6)
    for axis_at, shards_of in shards:
        draws = jnp.exp(jax.random.uniform(jax.random.fold_in(own, axis_at), (shards_of,), jnp.float32, least / len(shards), top_value / len(shards)))
        factor_of = factor_of * jnp.repeat(draws, shape[axis_at] // shards_of).reshape([-1 if axis == axis_at else 1 for axis in range(len(shape))])
    return factor_of


def centred(rng, extent, deviation, bound, shards=(), kind=jnp.bfloat16):
    entries = deviation * jax.random.normal(rng, extent, jnp.float32)
    if shards:
        entries = entries * block_levels(rng, extent, shards, -0.22, 0.18)
    return jnp.clip(entries, -bound, bound).astype(kind)


def setup_inputs(seed: int = 0) -> dict:
    arg_keys = jax.random.split(jax.random.key(seed), 5)
    return {
        "weights": centred(arg_keys[0], (N_RX, N_RY, 3, SLAB, D), 1.0, 6.0, ((0, 16), (1, 4), (3, 8))),
        "tracker": centred(arg_keys[1], (N_RX, N_RY, 3, SLAB, D), 1.0, 6.0, ((0, 16), (1, 4), (3, 8))),
        "acts": centred(arg_keys[2], (N_RX, N_RY, TOKENS, D), 1.0, 6.0, ((0, 16), (1, 4), (2, 8))),
        "cotangent": centred(arg_keys[3], (N_RX, N_RY, TOKENS, D), 1.0, 6.0, ((0, 16), (1, 4), (2, 8))),
    }


learning_rate = 0.1


def replica_gradient(inputs):
    slab_weights, token_rows, cotangent_rows = inputs
    input_scale = D ** -0.5
    output_scale = SLAB ** -0.5
    gate_pre = jnp.dot(token_rows, slab_weights[0].T, preferred_element_type=jnp.float32) * input_scale
    up_pre = jnp.dot(token_rows, slab_weights[1].T, preferred_element_type=jnp.float32) * input_scale
    sigmoid_gate = jax.nn.sigmoid(gate_pre)
    gated = gate_pre * sigmoid_gate
    hidden = (gated * up_pre).astype(jnp.bfloat16)
    hidden_grad = jnp.dot(cotangent_rows, slab_weights[2].T, preferred_element_type=jnp.float32) * output_scale
    up_grad = (hidden_grad * gated).astype(jnp.bfloat16)
    gate_grad = (hidden_grad * up_pre * sigmoid_gate * (1.0 + gate_pre * (1.0 - sigmoid_gate))).astype(jnp.bfloat16)

    def group_term(group_inputs):
        gate_part, up_part, hidden_part, token_part, cotangent_part = group_inputs
        gate_term = jnp.dot(gate_part.T, token_part, preferred_element_type=jnp.float32) * input_scale
        up_term = jnp.dot(up_part.T, token_part, preferred_element_type=jnp.float32) * input_scale
        down_term = jnp.dot(hidden_part.T, cotangent_part, preferred_element_type=jnp.float32) * output_scale
        return jnp.stack([gate_term, up_term, down_term], axis=0).astype(jnp.bfloat16)

    def split_groups(values):
        return values.reshape(N_TP, TOK_DEV, values.shape[1])

    grouped = tuple(split_groups(values) for values in (gate_grad, up_grad, hidden, token_rows, cotangent_rows))
    terms = lax.map(group_term, grouped)
    return jnp.sum(terms.astype(jnp.float32), axis=0).astype(jnp.bfloat16)


def torus_mean(field):
    values = field.astype(jnp.float32)
    total = values + jnp.roll(values, 1, 0) + jnp.roll(values, -1, 0)
    total = total + jnp.roll(values, 1, 1) + jnp.roll(values, -1, 1)
    return total / 5.0


def flatten_replicas(values):
    return values.reshape((N_RX * N_RY,) + values.shape[2:])


def reference(weights, tracker, acts, cotangent):
    gradient = lax.map(replica_gradient, (flatten_replicas(weights), flatten_replicas(acts), flatten_replicas(cotangent)))
    gradient = gradient.reshape(weights.shape)
    tracked = tracker.astype(jnp.float32) + gradient.astype(jnp.float32)
    new_weights = (torus_mean(weights) - learning_rate * tracked).astype(jnp.bfloat16)
    new_tracker = (torus_mean(tracker) + torus_mean(gradient) - gradient.astype(jnp.float32)).astype(jnp.bfloat16)
    return new_weights, new_tracker
```

```python
import functools

import jax
import jax.numpy as jnp
from jax import lax
from jax.experimental import pallas as pl
from jax.experimental.pallas import tpu as pltpu
from jax.sharding import PartitionSpec as P

MESH = pl.DeviceIdType.MESH

learning_rate = 0.1
chunks = 4
hop_slots = 2
first_slot = 1
far_slot = 2


def kernel(
    sizes,
    scales,
    part_rows,
    acts_hbm,
    cotangent_hbm,
    weights_hbm,
    tracker_hbm,
    new_weights_ref,
    new_tracker_ref,
    tokens,
    blocks,
    partials,
    from_left,
    from_right,
    tracker,
    gradient,
    outgoing,
    near_weights,
    near_tracked,
    load_sem,
    block_recv,
    block_send,
    own_send,
    left_recv,
    left_send,
    right_recv,
    right_send,
    mix_recv,
    mix_send,
    tracked_recv,
    tracked_send,
):
    n_rx, n_ry, n_tp = sizes
    input_scale, output_scale = scales
    rx = lax.axis_index("rx")
    ry = lax.axis_index("ry")
    me = lax.axis_index("tp")
    last = n_tp - 1
    has_left = me > 0
    has_right = me < last
    torus = (
        (lax.rem(rx + 1, n_rx), ry, me),
        (lax.rem(rx + n_rx - 1, n_rx), ry, me),
        (rx, lax.rem(ry + 1, n_ry), me),
        (rx, lax.rem(ry + n_ry - 1, n_ry), me),
    )
    to_left = (rx, ry, me - 1)
    to_right = (rx, ry, me + 1)
    here = (rx, ry, me)

    barrier = pltpu.get_barrier_semaphore()
    for partner in torus:
        pl.semaphore_signal(barrier, inc=1, device_id=partner, device_id_type=MESH)

    @pl.when(has_left)
    def _():
        pl.semaphore_signal(barrier, inc=1, device_id=to_left, device_id_type=MESH)

    @pl.when(has_right)
    def _():
        pl.semaphore_signal(barrier, inc=1, device_id=to_right, device_id_type=MESH)

    token_rows = acts_hbm.shape[0]
    loads = (
        pltpu.make_async_copy(weights_hbm, blocks.at[me], load_sem.at[0]),
        pltpu.make_async_copy(acts_hbm, tokens.at[pl.ds(0, token_rows)], load_sem.at[1]),
        pltpu.make_async_copy(cotangent_hbm, tokens.at[pl.ds(token_rows, token_rows)], load_sem.at[2]),
        pltpu.make_async_copy(tracker_hbm, tracker, load_sem.at[3]),
    )
    for load in loads:
        load.start()

    def send(source, target, send_sem, recv_sem, device):
        return pltpu.make_async_remote_copy(
            src_ref=source,
            dst_ref=target,
            send_sem=send_sem,
            recv_sem=recv_sem,
            device_id=device,
            device_id_type=MESH,
        )

    def block_copy(j, c, device):
        block = blocks.at[j, c]
        return send(block, block, block_send.at[j, c], block_recv.at[j, c], device)

    def own_copy(c):
        block = blocks.at[me, c]
        return send(block, block, own_send.at[c], block_recv.at[me, c], to_left)

    def rightward(j, c, device):
        block = from_left.at[j, c]
        return send(block, block, left_send.at[j, c], left_recv.at[j, c], device)

    def leftward(j, c, device):
        block = from_right.at[j, c]
        return send(block, block, right_send.at[j, c], right_recv.at[j, c], device)

    def mix_copy(k, device):
        return send(blocks.at[me], near_weights.at[k ^ 1], mix_send.at[k], mix_recv.at[k ^ 1], device)

    def tracked_copy(k, c, device):
        return send(
            outgoing.at[c], near_tracked.at[k ^ 1, c], tracked_send.at[k, c], tracked_recv.at[k ^ 1, c], device
        )

    loads[0].wait()
    pl.semaphore_wait(barrier, 4 + has_left.astype(jnp.int32) + has_right.astype(jnp.int32))

    for c in range(chunks):

        @pl.when(has_left)
        def _():
            own_copy(c).start()

        @pl.when(has_right)
        def _():
            block_copy(me, c, to_right).start()

    for k in (2, 3, 0, 1):
        mix_copy(k, torus[k]).start()

    for load in loads[1:]:
        load.wait()

    width = blocks.shape[3]
    rows = blocks.shape[2]
    row = lax.broadcasted_iota(jnp.int32, (rows, token_rows), 0)
    is_gate = row < part_rows
    is_up = (row >= part_rows) & (row < 2 * part_rows)
    is_down = (row >= 2 * part_rows) & (row < 3 * part_rows)
    row_scale = jnp.where(
        lax.broadcasted_iota(jnp.int32, (rows, 1), 0) < 2 * part_rows, input_scale, output_scale
    ).astype(jnp.float32)

    def compute(j):
        pre = jnp.zeros((rows, 2 * token_rows), jnp.float32)
        for c in range(chunks):
            pre += lax.dot_general(
                blocks[j, c],
                tokens[:, c * width : (c + 1) * width],
                (((1,), (1,)), ((), ())),
                preferred_element_type=jnp.float32,
            )
        gate = pre[:, :token_rows] * input_scale
        up = pltpu.roll(pre[:, :token_rows], rows - part_rows, 0) * input_scale
        hidden_grad = pltpu.roll(pre[:, token_rows:], rows - 2 * part_rows, 0) * output_scale
        sigmoid_gate = jax.nn.sigmoid(gate)
        gated = gate * sigmoid_gate
        hidden = gated * up
        up_grad = hidden_grad * gated
        gate_grad = hidden_grad * up * sigmoid_gate * (1.0 + gate * (1.0 - sigmoid_gate))
        with_tokens = jnp.where(is_gate, gate_grad, jnp.where(is_up, pltpu.roll(up_grad, part_rows, 0), 0.0))
        with_cotangent = jnp.where(is_down, pltpu.roll(hidden, 2 * part_rows, 0), 0.0)
        both = jnp.concatenate([with_tokens, with_cotangent], axis=1).astype(jnp.bfloat16)
        for c in range(chunks):
            partials[j, c] = (
                jnp.dot(both, tokens[:, c * width : (c + 1) * width], preferred_element_type=jnp.float32) * row_scale
            )

    start_right = first_slot + (chunks + hop_slots) * me
    start_left = first_slot + (chunks + hop_slots) * (last - me)
    finish = jnp.maximum(start_right, start_left)

    @pl.loop(0, first_slot + (chunks + hop_slots) * last + chunks)
    def _(slot):
        arrived = slot - first_slot + chunks
        distance = lax.div(arrived, chunks)
        c = lax.rem(arrived, chunks)

        @pl.when((distance >= 1) & (me + distance <= last))
        def _():
            j = me + distance
            block_copy(j, c, here).wait_recv()

            @pl.when(has_left)
            def _():
                block_copy(j, c, to_left).start()

        @pl.when((distance >= 1) & (me - distance >= 0))
        def _():
            j = me - distance
            block_copy(j, c, here).wait_recv()

            @pl.when(has_right)
            def _():
                block_copy(j, c, to_right).start()

        @pl.when((c == chunks - 1) & (distance <= last))
        def _():
            @pl.loop(0, 2)
            def _(side):
                j = me + distance * (1 - 2 * side)

                @pl.when((j >= 0) & (j <= last) & (distance + 1 > side))
                def _():
                    compute(j)

        gone = slot - start_right + chunks
        ahead = lax.div(gone, chunks) - 1
        part = lax.rem(gone, chunks)

        @pl.when((gone >= 0) & (ahead >= 1) & (me + ahead <= last))
        def _():
            j = me + ahead

            @pl.when(has_left)
            def _():
                rightward(j, part, here).wait_recv()
                from_left[j, part] = (from_left[j, part].astype(jnp.float32) + partials[j, part]).astype(jnp.bfloat16)

            @pl.when(jnp.logical_not(has_left))
            def _():
                from_left[j, part] = partials[j, part].astype(jnp.bfloat16)

            rightward(j, part, to_right).start()

        gone_left = slot - start_left + chunks
        behind = lax.div(gone_left, chunks) - 1
        piece = lax.rem(gone_left, chunks)

        @pl.when((gone_left >= 0) & (behind >= 1) & (me - behind >= 0))
        def _():
            j = me - behind

            @pl.when(has_right)
            def _():
                leftward(j, piece, here).wait_recv()
                from_right[j, piece] = (from_right[j, piece].astype(jnp.float32) + partials[j, piece]).astype(
                    jnp.bfloat16
                )

            @pl.when(jnp.logical_not(has_right))
            def _():
                from_right[j, piece] = partials[j, piece].astype(jnp.bfloat16)

            leftward(j, piece, to_left).start()

        done = slot - finish

        @pl.when((done >= 0) & (done < chunks))
        def _():
            @pl.when(has_left)
            def _():
                rightward(me, done, here).wait_recv()
                partials[me, done] = partials[me, done] + from_left[me, done].astype(jnp.float32)

            @pl.when(has_right)
            def _():
                leftward(me, done, here).wait_recv()
                partials[me, done] = partials[me, done] + from_right[me, done].astype(jnp.float32)

            rounded = partials[me, done].astype(jnp.bfloat16)
            gradient[done] = rounded
            outgoing[done] = (tracker[done].astype(jnp.float32) + rounded.astype(jnp.float32)).astype(jnp.bfloat16)
            for k in range(4):
                tracked_copy(k, done, torus[k]).start()

    for k in range(4):
        mix_copy(k ^ 1, here).wait_recv()

    @pl.loop(0, chunks)
    def _(c):
        for k in range(4):
            tracked_copy(k ^ 1, c, here).wait_recv()
        own_gradient = gradient[c].astype(jnp.float32)
        tracked = tracker[c].astype(jnp.float32) + own_gradient
        weight_sum = blocks[me, c].astype(jnp.float32)
        tracked_sum = tracked
        for k in range(4):
            weight_sum = weight_sum + near_weights[k, c].astype(jnp.float32)
            tracked_sum = tracked_sum + near_tracked[k, c].astype(jnp.float32)
        new_weights_ref[c] = (weight_sum * 0.2 - learning_rate * tracked).astype(jnp.bfloat16)
        new_tracker_ref[c] = (tracked_sum * 0.2 - own_gradient).astype(jnp.bfloat16)

    for k in range(4):
        mix_copy(k, torus[k]).wait_send()

    @pl.loop(0, chunks)
    def _(c):
        for k in range(4):
            tracked_copy(k, c, torus[k]).wait_send()

        @pl.when(has_left)
        def _():
            own_copy(c).wait_send()

        @pl.when(has_right)
        def _():
            block_copy(me, c, here).wait_send()

        @pl.loop(0, n_tp)
        def _(j):
            @pl.when(((j > me) & has_left) | ((j < me) & has_right))
            def _():
                block_copy(j, c, here).wait_send()

            @pl.when(j > me)
            def _():
                rightward(j, c, here).wait_send()

            @pl.when(j < me)
            def _():
                leftward(j, c, here).wait_send()


def on_device(sizes, weights, tracker, acts, cotangent):
    _, _, matrices, part_rows, model_width = weights.shape
    n_tp = sizes[2]
    used = matrices * part_rows
    rows = -(-used // 16) * 16
    width = model_width // chunks
    token_rows = acts.shape[2]

    def packed(values):
        flat = values.reshape(used, chunks, width)
        flat = jnp.pad(flat, ((0, rows - used), (0, 0), (0, 0)))
        return flat.transpose(1, 0, 2)

    def unpacked(values):
        return values.transpose(1, 0, 2)[:used].reshape(weights.shape)

    scales = (model_width ** (-0.5), (part_rows * n_tp) ** (-0.5))
    shape = (chunks, rows, width)
    half = jnp.bfloat16
    dma = pltpu.SemaphoreType.DMA
    new_weights, new_tracker = pl.pallas_call(
        functools.partial(kernel, sizes, scales, part_rows),
        out_shape=[jax.ShapeDtypeStruct(shape, half)] * 2,
        in_specs=[pl.BlockSpec(memory_space=pl.ANY)] * 4,
        out_specs=[pl.BlockSpec(memory_space=pltpu.VMEM)] * 2,
        scratch_shapes=[
            pltpu.VMEM((2 * token_rows, model_width), half),
            pltpu.VMEM((n_tp, *shape), half),
            pltpu.VMEM((n_tp, *shape), jnp.float32),
            pltpu.VMEM((n_tp, *shape), half),
            pltpu.VMEM((n_tp, *shape), half),
            pltpu.VMEM(shape, half),
            pltpu.VMEM(shape, half),
            pltpu.VMEM(shape, half),
            pltpu.VMEM((4, *shape), half),
            pltpu.VMEM((4, *shape), half),
            dma((4,)),
            dma((n_tp, chunks)),
            dma((n_tp, chunks)),
            dma((chunks,)),
            dma((n_tp, chunks)),
            dma((n_tp, chunks)),
            dma((n_tp, chunks)),
            dma((n_tp, chunks)),
            dma((4,)),
            dma((4,)),
            dma((4, chunks)),
            dma((4, chunks)),
        ],
        compiler_params=pltpu.CompilerParams(
            collective_id=0, has_side_effects=True, vmem_limit_bytes=48 * 1024 * 1024
        ),
        cost_estimate=pl.CostEstimate(flops=2_000_000_000, bytes_accessed=8_000_000, transcendentals=100_000),
    )(acts[0, 0], cotangent[0, 0], packed(weights), packed(tracker))
    return unpacked(new_weights), unpacked(new_tracker)


def solution(mesh):
    sizes = tuple(mesh.shape[axis] for axis in ("rx", "ry", "tp"))
    rows_split = P("rx", "ry", None, "tp", None)
    tokens_split = P("rx", "ry", "tp", None)
    return jax.shard_map(
        functools.partial(on_device, sizes),
        mesh=mesh,
        in_specs=(rows_split, rows_split, tokens_split, tokens_split),
        out_specs=(rows_split, rows_split),
        check_vma=False,
    )
```

```python
import functools

import jax
import jax.numpy as jnp
from jax import lax
from jax.experimental import pallas as pl
from jax.experimental.pallas import tpu as pltpu
from jax.sharding import PartitionSpec as P

MESH = pl.DeviceIdType.MESH

learning_rate = 0.1
chunks = 8
hop_slots = 3
first_slot = 1


def kernel(
    sizes,
    scales,
    part_rows,
    acts_hbm,
    cotangent_hbm,
    weights_hbm,
    tracker_hbm,
    new_weights_ref,
    new_tracker_ref,
    tokens,
    blocks,
    partials,
    from_left,
    from_right,
    to_far,
    tracker,
    gradient,
    outgoing,
    near_weights,
    near_tracked,
    load_sem,
    block_recv,
    block_send,
    own_send,
    left_recv,
    left_send,
    right_recv,
    right_send,
    mix_recv,
    mix_send,
    tracked_recv,
    tracked_send,
    far_weights_recv,
    far_recv,
    far_send,
):
    n_rx, n_ry, n_tp = sizes
    input_scale, output_scale = scales
    rx = lax.axis_index("rx")
    ry = lax.axis_index("ry")
    me = lax.axis_index("tp")
    last = n_tp - 1
    has_left = me > 0
    has_right = me < last
    torus = (
        (lax.rem(rx + 1, n_rx), ry, me),
        (lax.rem(rx + n_rx - 1, n_rx), ry, me),
        (rx, lax.rem(ry + 1, n_ry), me),
        (rx, lax.rem(ry + n_ry - 1, n_ry), me),
    )
    to_left = (rx, ry, me - 1)
    to_right = (rx, ry, me + 1)
    here = (rx, ry, me)

    place = lax.rem(rx, n_rx // 2)
    is_first = place == 0
    is_last = place == n_rx // 2 - 1
    is_edge = is_first | is_last
    near = (jnp.logical_not(is_last), jnp.logical_not(is_first), rx >= 0, rx >= 0)
    far_rx = jnp.where(is_last, torus[0][0], torus[1][0])
    far_side = jnp.where(is_last, 0, 1)
    middle = n_tp // 2
    feeder = (far_rx, ry, jnp.where(me < middle, last, 0))

    barrier = pltpu.get_barrier_semaphore()
    for exists, partner in zip(near, torus):

        @pl.when(exists)
        def _():
            pl.semaphore_signal(barrier, inc=1, device_id=partner, device_id_type=MESH)

    @pl.when(is_edge)
    def _():
        pl.semaphore_signal(barrier, inc=1, device_id=feeder, device_id_type=MESH)

    @pl.when(has_left)
    def _():
        pl.semaphore_signal(barrier, inc=1, device_id=to_left, device_id_type=MESH)

    @pl.when(has_right)
    def _():
        pl.semaphore_signal(barrier, inc=1, device_id=to_right, device_id_type=MESH)

    token_rows = acts_hbm.shape[0]
    loads = (
        pltpu.make_async_copy(weights_hbm, blocks.at[me], load_sem.at[0]),
        pltpu.make_async_copy(acts_hbm, tokens.at[pl.ds(0, token_rows)], load_sem.at[1]),
        pltpu.make_async_copy(cotangent_hbm, tokens.at[pl.ds(token_rows, token_rows)], load_sem.at[2]),
        pltpu.make_async_copy(tracker_hbm, tracker, load_sem.at[3]),
    )
    for load in loads:
        load.start()

    def send(source, target, send_sem, recv_sem, device):
        return pltpu.make_async_remote_copy(
            src_ref=source,
            dst_ref=target,
            send_sem=send_sem,
            recv_sem=recv_sem,
            device_id=device,
            device_id_type=MESH,
        )

    def block_copy(j, c, device):
        block = blocks.at[j, c]
        return send(block, block, block_send.at[j, c], block_recv.at[j, c], device)

    def own_copy(c):
        block = blocks.at[me, c]
        return send(block, block, own_send.at[c], block_recv.at[me, c], to_left)

    def rightward(j, c, device):
        block = from_left.at[j, c]
        return send(block, block, left_send.at[j, c], left_recv.at[j, c], device)

    def leftward(j, c, device):
        block = from_right.at[j, c]
        return send(block, block, right_send.at[j, c], right_recv.at[j, c], device)

    def mix_copy(k, device):
        return send(blocks.at[me], near_weights.at[k ^ 1], mix_send.at[k], mix_recv.at[k ^ 1], device)

    def tracked_copy(k, c, device):
        return send(
            outgoing.at[c], near_tracked.at[k ^ 1, c], tracked_send.at[k, c], tracked_recv.at[k ^ 1, c], device
        )

    def far_weights_copy(j, c):
        return send(
            blocks.at[j, c],
            near_weights.at[1 - far_side, c],
            block_send.at[j, c],
            far_weights_recv.at[c],
            (far_rx, ry, j),
        )

    def far_copy(j, c, device):
        block = to_far.at[j, c]
        return send(block, block, far_send.at[j, c], far_recv.at[j, c], device)

    def last_far_copy(j, c):
        return send(
            to_far.at[j, c],
            near_tracked.at[1 - far_side, c],
            far_send.at[j, c],
            tracked_recv.at[1 - far_side, c],
            (far_rx, ry, j),
        )

    loads[0].wait()
    expected = (
        jnp.where(is_edge, 3, 4)
        + jnp.where(has_left, 1, 0)
        + jnp.where(has_right, 1, 0)
        + jnp.where(is_edge & (me == 0), n_tp - middle, 0)
        + jnp.where(is_edge & (me == last), middle, 0)
    )
    pl.semaphore_wait(barrier, expected)

    for c in range(chunks):

        @pl.when(has_left)
        def _():
            own_copy(c).start()

        @pl.when(has_right)
        def _():
            block_copy(me, c, to_right).start()

    for k in (2, 3, 0, 1):

        @pl.when(near[k])
        def _():
            mix_copy(k, torus[k]).start()

    for load in loads[1:]:
        load.wait()

    width = blocks.shape[3]
    rows = blocks.shape[2]
    row = lax.broadcasted_iota(jnp.int32, (rows, token_rows), 0)
    is_gate = row < part_rows
    is_up = (row >= part_rows) & (row < 2 * part_rows)
    is_down = (row >= 2 * part_rows) & (row < 3 * part_rows)
    row_scale = jnp.where(
        lax.broadcasted_iota(jnp.int32, (rows, 1), 0) < 2 * part_rows, input_scale, output_scale
    ).astype(jnp.float32)

    def compute(j):
        pre = jnp.zeros((rows, 2 * token_rows), jnp.float32)
        for c in range(chunks):
            pre += lax.dot_general(
                blocks[j, c],
                tokens[:, c * width : (c + 1) * width],
                (((1,), (1,)), ((), ())),
                preferred_element_type=jnp.float32,
            )
        gate = pre[:, :token_rows] * input_scale
        up = pltpu.roll(pre[:, :token_rows], rows - part_rows, 0) * input_scale
        hidden_grad = pltpu.roll(pre[:, token_rows:], rows - 2 * part_rows, 0) * output_scale
        sigmoid_gate = jax.nn.sigmoid(gate)
        gated = gate * sigmoid_gate
        hidden = gated * up
        up_grad = hidden_grad * gated
        gate_grad = hidden_grad * up * sigmoid_gate * (1.0 + gate * (1.0 - sigmoid_gate))
        with_tokens = jnp.where(is_gate, gate_grad, jnp.where(is_up, pltpu.roll(up_grad, part_rows, 0), 0.0))
        with_cotangent = jnp.where(is_down, pltpu.roll(hidden, 2 * part_rows, 0), 0.0)
        both = jnp.concatenate([with_tokens, with_cotangent], axis=1).astype(jnp.bfloat16)
        for c in range(chunks):
            partials[j, c] = (
                jnp.dot(both, tokens[:, c * width : (c + 1) * width], preferred_element_type=jnp.float32) * row_scale
            )

    start_right = first_slot + (chunks + hop_slots) * me
    start_left = first_slot + (chunks + hop_slots) * (last - me)
    finish = jnp.maximum(start_right, start_left)

    @pl.loop(0, first_slot + (chunks + hop_slots) * last + chunks)
    def _(slot):
        arrived = slot - first_slot + chunks
        distance = lax.div(arrived, chunks)
        c = lax.rem(arrived, chunks)

        @pl.when((distance >= 1) & (me + distance <= last))
        def _():
            j = me + distance
            block_copy(j, c, here).wait_recv()

            @pl.when(has_left)
            def _():
                block_copy(j, c, to_left).start()

            @pl.when(is_edge & jnp.logical_not(has_left) & (j >= middle))
            def _():
                far_weights_copy(j, c).start()

        @pl.when((distance >= 1) & (me - distance >= 0))
        def _():
            j = me - distance
            block_copy(j, c, here).wait_recv()

            @pl.when(has_right)
            def _():
                block_copy(j, c, to_right).start()

            @pl.when(is_edge & jnp.logical_not(has_right) & (j < middle))
            def _():
                far_weights_copy(j, c).start()

        @pl.when((c == chunks - 1) & (distance <= last))
        def _():
            @pl.loop(0, 2)
            def _(side):
                j = me + distance * (1 - 2 * side)

                @pl.when((j >= 0) & (j <= last) & (distance + 1 > side))
                def _():
                    compute(j)

        gone = slot - start_right + chunks
        ahead = lax.div(gone, chunks) - 1
        part = lax.rem(gone, chunks)

        @pl.when((gone >= 0) & (ahead >= 1) & (me + ahead <= last))
        def _():
            j = me + ahead

            @pl.when(has_left)
            def _():
                rightward(j, part, here).wait_recv()
                from_left[j, part] = (from_left[j, part].astype(jnp.float32) + partials[j, part]).astype(jnp.bfloat16)

            @pl.when(jnp.logical_not(has_left))
            def _():
                from_left[j, part] = partials[j, part].astype(jnp.bfloat16)

            rightward(j, part, to_right).start()

        gone_left = slot - start_left + chunks
        behind = lax.div(gone_left, chunks) - 1
        piece = lax.rem(gone_left, chunks)

        @pl.when((gone_left >= 0) & (behind >= 1) & (me - behind >= 0))
        def _():
            j = me - behind

            @pl.when(has_right)
            def _():
                leftward(j, piece, here).wait_recv()
                from_right[j, piece] = (from_right[j, piece].astype(jnp.float32) + partials[j, piece]).astype(
                    jnp.bfloat16
                )

            @pl.when(jnp.logical_not(has_right))
            def _():
                from_right[j, piece] = partials[j, piece].astype(jnp.bfloat16)

            leftward(j, piece, to_left).start()

        @pl.when(has_left & (gone >= chunks) & (gone < 2 * chunks))
        def _():
            rightward(me, part, here).wait_recv()
            partials[me, part] = partials[me, part] + from_left[me, part].astype(jnp.float32)

        @pl.when(has_right & (gone_left >= chunks) & (gone_left < 2 * chunks))
        def _():
            leftward(me, piece, here).wait_recv()
            partials[me, piece] = partials[me, piece] + from_right[me, piece].astype(jnp.float32)

        @pl.when(is_edge)
        def _():
            @pl.loop(0, n_tp)
            def _(j):
                goes_right = j < middle
                hops = jnp.where(goes_right, me - j, j - me)
                begun = (chunks + hop_slots) * jnp.where(goes_right, j, last - j)
                at = slot - first_slot - jnp.maximum(begun + hop_slots * hops, chunks * hops)

                @pl.when((hops >= 0) & (at >= 0) & (at < chunks))
                def _():
                    @pl.when(hops == 0)
                    def _():
                        to_far[j, at] = (tracker[at].astype(jnp.float32) + partials[j, at]).astype(jnp.bfloat16)

                    @pl.when(hops > 0)
                    def _():
                        far_copy(j, at, here).wait_recv()
                        to_far[j, at] = (to_far[j, at].astype(jnp.float32) + partials[j, at]).astype(jnp.bfloat16)

                    ends = jnp.where(goes_right, me == last, me == 0)

                    @pl.when(ends)
                    def _():
                        last_far_copy(j, at).start()

                    @pl.when(jnp.logical_not(ends))
                    def _():
                        far_copy(j, at, (rx, ry, jnp.where(goes_right, me + 1, me - 1))).start()

        done = slot - finish

        @pl.when((done >= 0) & (done < chunks))
        def _():
            rounded = partials[me, done].astype(jnp.bfloat16)
            gradient[done] = rounded
            outgoing[done] = (tracker[done].astype(jnp.float32) + rounded.astype(jnp.float32)).astype(jnp.bfloat16)
            for k in (0, 1, 2, 3):

                @pl.when(near[k])
                def _():
                    tracked_copy(k, done, torus[k]).start()

    for k in range(4):

        @pl.when(near[k])
        def _():
            mix_copy(k ^ 1, here).wait_recv()

    @pl.when(is_edge)
    def _():
        @pl.loop(0, chunks)
        def _(c):
            landed = near_weights.at[far_side, c]
            send(landed, landed, far_send.at[0, c], far_weights_recv.at[c], here).wait_recv()

    @pl.loop(0, chunks)
    def _(c):
        for k in range(4):
            tracked_copy(k ^ 1, c, here).wait_recv()
        own_gradient = gradient[c].astype(jnp.float32)
        tracked = tracker[c].astype(jnp.float32) + own_gradient
        weight_sum = blocks[me, c].astype(jnp.float32)
        tracked_sum = tracked
        for k in range(4):
            weight_sum = weight_sum + near_weights[k, c].astype(jnp.float32)
            tracked_sum = tracked_sum + near_tracked[k, c].astype(jnp.float32)
        new_weights_ref[c] = (weight_sum * 0.2 - learning_rate * tracked).astype(jnp.bfloat16)
        new_tracker_ref[c] = (tracked_sum * 0.2 - own_gradient).astype(jnp.bfloat16)

    for k in range(4):

        @pl.when(near[k])
        def _():
            mix_copy(k, torus[k]).wait_send()

    @pl.loop(0, chunks)
    def _(c):
        for k in range(4):

            @pl.when(near[k])
            def _():
                tracked_copy(k, c, torus[k]).wait_send()

        @pl.when(has_left)
        def _():
            own_copy(c).wait_send()

        @pl.when(has_right)
        def _():
            block_copy(me, c, here).wait_send()

        @pl.loop(0, n_tp)
        def _(j):
            passed = ((j > me) & has_left) | ((j < me) & has_right)
            farther = ((j >= middle) & (me == 0)) | ((j < middle) & (me == last))

            @pl.when(passed | (is_edge & farther))
            def _():
                block_copy(j, c, here).wait_send()

            @pl.when(is_edge & (((j < middle) & (j <= me)) | ((j >= middle) & (j >= me))))
            def _():
                far_copy(j, c, here).wait_send()

            @pl.when(j > me)
            def _():
                rightward(j, c, here).wait_send()

            @pl.when(j < me)
            def _():
                leftward(j, c, here).wait_send()


def on_device(sizes, weights, tracker, acts, cotangent):
    _, _, matrices, part_rows, model_width = weights.shape
    n_tp = sizes[2]
    used = matrices * part_rows
    rows = -(-used // 16) * 16
    width = model_width // chunks
    token_rows = acts.shape[2]

    def packed(values):
        flat = values.reshape(used, chunks, width)
        flat = jnp.pad(flat, ((0, rows - used), (0, 0), (0, 0)))
        return flat.transpose(1, 0, 2)

    def unpacked(values):
        return values.transpose(1, 0, 2)[:used].reshape(weights.shape)

    scales = (model_width ** (-0.5), (part_rows * n_tp) ** (-0.5))
    shape = (chunks, rows, width)
    half = jnp.bfloat16
    dma = pltpu.SemaphoreType.DMA
    new_weights, new_tracker = pl.pallas_call(
        functools.partial(kernel, sizes, scales, part_rows),
        out_shape=[jax.ShapeDtypeStruct(shape, half)] * 2,
        in_specs=[pl.BlockSpec(memory_space=pl.ANY)] * 4,
        out_specs=[pl.BlockSpec(memory_space=pltpu.VMEM)] * 2,
        scratch_shapes=[
            pltpu.VMEM((2 * token_rows, model_width), half),
            pltpu.VMEM((n_tp, *shape), half),
            pltpu.VMEM((n_tp, *shape), jnp.float32),
            pltpu.VMEM((n_tp, *shape), half),
            pltpu.VMEM((n_tp, *shape), half),
            pltpu.VMEM((n_tp, *shape), half),
            pltpu.VMEM(shape, half),
            pltpu.VMEM(shape, half),
            pltpu.VMEM(shape, half),
            pltpu.VMEM((4, *shape), half),
            pltpu.VMEM((4, *shape), half),
            dma((4,)),
            dma((n_tp, chunks)),
            dma((n_tp, chunks)),
            dma((chunks,)),
            dma((n_tp, chunks)),
            dma((n_tp, chunks)),
            dma((n_tp, chunks)),
            dma((n_tp, chunks)),
            dma((4,)),
            dma((4,)),
            dma((4, chunks)),
            dma((4, chunks)),
            dma((chunks,)),
            dma((n_tp, chunks)),
            dma((n_tp, chunks)),
        ],
        compiler_params=pltpu.CompilerParams(
            collective_id=0, has_side_effects=True, vmem_limit_bytes=48 * 1024 * 1024
        ),
        cost_estimate=pl.CostEstimate(flops=2_000_000_000, bytes_accessed=8_000_000, transcendentals=100_000),
    )(acts[0, 0], cotangent[0, 0], packed(weights), packed(tracker))
    return unpacked(new_weights), unpacked(new_tracker)


def solution(mesh):
    sizes = tuple(mesh.shape[axis] for axis in ("rx", "ry", "tp"))
    rows_split = P("rx", "ry", None, "tp", None)
    tokens_split = P("rx", "ry", "tp", None)
    return jax.shard_map(
        functools.partial(on_device, sizes),
        mesh=mesh,
        in_specs=(rows_split, rows_split, tokens_split, tokens_split),
        out_specs=(rows_split, rows_split),
        check_vma=False,
    )
```

```python
import functools

import jax
import jax.numpy as jnp
from jax import lax
from jax.experimental import pallas as pl
from jax.experimental.pallas import tpu as pltpu
from jax.sharding import PartitionSpec as P

MESH = pl.DeviceIdType.MESH

learning_rate = 0.1
chunks = 8
hop_slots = 4
compute_slots = 2
arrival_order = (1, 2, 3, 7, 6, 5, 4)


def timetable(n_tp):
    last = n_tp - 1
    sent, arrived, summed, far = {}, {}, {}, {}
    for p in range(last, -1, -1):
        free = 0
        for j in arrival_order + (0,):
            if j < p:
                continue
            slot = max(free, 0 if j == p else sent[p + 1, j] + hop_slots)
            if p == 0 and j > 0:
                slot = sent[1, j] + hop_slots
            sent[p, j] = slot
            free = slot + chunks
    for p in range(n_tp):
        free = 0
        for j in arrival_order:
            if j <= p:
                continue
            slot = max(free, sent[p, j] + chunks - 1 + compute_slots)
            if p > 0:
                slot = max(slot, summed[p - 1, j] + hop_slots)
            summed[p, j] = slot
            free = slot + chunks
    for j in range(n_tp):
        summed[j, j] = summed[j - 1, j] + hop_slots if j else 0
    for j in range(n_tp // 2):
        far[j, j] = summed[j, j]
        for p in range(j + 1, n_tp):
            far[p, j] = max(far[p - 1, j] + hop_slots, sent[last - p, last - j] + chunks - 1 + compute_slots)
    return sent, summed, far


def kernel(
    sizes,
    scales,
    part_rows,
    acts_hbm,
    cotangent_hbm,
    weights_hbm,
    tracker_hbm,
    new_weights_ref,
    new_tracker_ref,
    tokens,
    blocks,
    partials,
    from_left,
    from_right,
    to_far,
    tracker,
    gradient,
    outgoing,
    near_weights,
    near_tracked,
    load_sem,
    block_recv,
    block_send,
    own_send,
    left_recv,
    left_send,
    right_recv,
    right_send,
    mix_recv,
    mix_send,
    tracked_recv,
    tracked_send,
    far_weights_recv,
    far_recv,
    far_send,
):
    n_rx, n_ry, n_tp = sizes
    input_scale, output_scale = scales
    rx = lax.axis_index("rx")
    ry = lax.axis_index("ry")
    me = lax.axis_index("tp")
    last = n_tp - 1
    has_left = me > 0
    has_right = me < last
    torus = (
        (lax.rem(rx + 1, n_rx), ry, me),
        (lax.rem(rx + n_rx - 1, n_rx), ry, me),
        (rx, lax.rem(ry + 1, n_ry), me),
        (rx, lax.rem(ry + n_ry - 1, n_ry), me),
    )
    to_left = (rx, ry, me - 1)
    to_right = (rx, ry, me + 1)
    here = (rx, ry, me)

    place = lax.rem(rx, n_rx // 2)
    is_first = place == 0
    is_last = place == n_rx // 2 - 1
    is_edge = is_first | is_last
    near = (jnp.logical_not(is_last), jnp.logical_not(is_first), rx >= 0, rx >= 0)
    far_rx = jnp.where(is_last, torus[0][0], torus[1][0])
    far_side = jnp.where(is_last, 0, 1)
    middle = n_tp // 2
    feeder = (far_rx, ry, jnp.where(me < middle, last, 0))

    barrier = pltpu.get_barrier_semaphore()
    for exists, partner in zip(near, torus):

        @pl.when(exists)
        def _():
            pl.semaphore_signal(barrier, inc=1, device_id=partner, device_id_type=MESH)

    @pl.when(is_edge)
    def _():
        pl.semaphore_signal(barrier, inc=1, device_id=feeder, device_id_type=MESH)

    @pl.when(has_left)
    def _():
        pl.semaphore_signal(barrier, inc=1, device_id=to_left, device_id_type=MESH)

    @pl.when(has_right)
    def _():
        pl.semaphore_signal(barrier, inc=1, device_id=to_right, device_id_type=MESH)

    token_rows = acts_hbm.shape[0]
    loads = (
        pltpu.make_async_copy(weights_hbm, blocks.at[me], load_sem.at[0]),
        pltpu.make_async_copy(acts_hbm, tokens.at[pl.ds(0, token_rows)], load_sem.at[1]),
        pltpu.make_async_copy(cotangent_hbm, tokens.at[pl.ds(token_rows, token_rows)], load_sem.at[2]),
        pltpu.make_async_copy(tracker_hbm, tracker, load_sem.at[3]),
    )
    for load in loads:
        load.start()

    def send(source, target, send_sem, recv_sem, device):
        return pltpu.make_async_remote_copy(
            src_ref=source,
            dst_ref=target,
            send_sem=send_sem,
            recv_sem=recv_sem,
            device_id=device,
            device_id_type=MESH,
        )

    def block_copy(j, c, device):
        block = blocks.at[j, c]
        return send(block, block, block_send.at[j, c], block_recv.at[j, c], device)

    def own_copy(c):
        block = blocks.at[me, c]
        return send(block, block, own_send.at[c], block_recv.at[me, c], to_left)

    def rightward(j, c, device):
        block = from_left.at[j, c]
        return send(block, block, left_send.at[j, c], left_recv.at[j, c], device)

    def leftward(j, c, device):
        block = from_right.at[j, c]
        return send(block, block, right_send.at[j, c], right_recv.at[j, c], device)

    def mix_copy(k, device):
        return send(blocks.at[me], near_weights.at[k ^ 1], mix_send.at[k], mix_recv.at[k ^ 1], device)

    def tracked_copy(k, c, device):
        return send(
            outgoing.at[c], near_tracked.at[k ^ 1, c], tracked_send.at[k, c], tracked_recv.at[k ^ 1, c], device
        )

    def far_weights_copy(j, c):
        return send(
            blocks.at[j, c],
            near_weights.at[1 - far_side, c],
            block_send.at[j, c],
            far_weights_recv.at[c],
            (far_rx, ry, j),
        )

    def far_copy(j, c, device):
        block = to_far.at[j, c]
        return send(block, block, far_send.at[j, c], far_recv.at[j, c], device)

    def last_far_copy(j, c):
        return send(
            to_far.at[j, c],
            near_tracked.at[1 - far_side, c],
            far_send.at[j, c],
            tracked_recv.at[1 - far_side, c],
            (far_rx, ry, j),
        )

    loads[0].wait()
    expected = (
        jnp.where(is_edge, 3, 4)
        + jnp.where(has_left, 1, 0)
        + jnp.where(has_right, 1, 0)
        + jnp.where(is_edge & (me == 0), n_tp - middle, 0)
        + jnp.where(is_edge & (me == last), middle, 0)
    )
    pl.semaphore_wait(barrier, expected)

    for k in (2, 3, 0, 1):

        @pl.when(near[k])
        def _():
            mix_copy(k, torus[k]).start()

    for load in loads[1:]:
        load.wait()

    width = blocks.shape[3]
    rows = blocks.shape[2]
    row = lax.broadcasted_iota(jnp.int32, (rows, token_rows), 0)
    is_gate = row < part_rows
    is_up = (row >= part_rows) & (row < 2 * part_rows)
    is_down = (row >= 2 * part_rows) & (row < 3 * part_rows)
    row_scale = jnp.where(
        lax.broadcasted_iota(jnp.int32, (rows, 1), 0) < 2 * part_rows, input_scale, output_scale
    ).astype(jnp.float32)

    def compute(j):
        pre = jnp.zeros((rows, 2 * token_rows), jnp.float32)
        for c in range(chunks):
            pre += lax.dot_general(
                blocks[j, c],
                tokens[:, c * width : (c + 1) * width],
                (((1,), (1,)), ((), ())),
                preferred_element_type=jnp.float32,
            )
        gate = pre[:, :token_rows] * input_scale
        up = pltpu.roll(pre[:, :token_rows], rows - part_rows, 0) * input_scale
        hidden_grad = pltpu.roll(pre[:, token_rows:], rows - 2 * part_rows, 0) * output_scale
        sigmoid_gate = jax.nn.sigmoid(gate)
        gated = gate * sigmoid_gate
        hidden = gated * up
        up_grad = hidden_grad * gated
        gate_grad = hidden_grad * up * sigmoid_gate * (1.0 + gate * (1.0 - sigmoid_gate))
        with_tokens = jnp.where(is_gate, gate_grad, jnp.where(is_up, pltpu.roll(up_grad, part_rows, 0), 0.0))
        with_cotangent = jnp.where(is_down, pltpu.roll(hidden, 2 * part_rows, 0), 0.0)
        both = jnp.concatenate([with_tokens, with_cotangent], axis=1).astype(jnp.bfloat16)
        for c in range(chunks):
            partials[j, c] = (
                jnp.dot(both, tokens[:, c * width : (c + 1) * width], preferred_element_type=jnp.float32) * row_scale
            )

    sent, summed, far = timetable(n_tp)

    def at_me(values):
        chosen = jnp.int32(values[0])
        for p in range(1, n_tp):
            chosen = jnp.where(me == p, values[p], chosen)
        return chosen

    devices = range(n_tp)
    own_left = at_me([sent[p, p] for p in devices])
    own_right = at_me([sent[last - p, last - p] for p in devices])
    arrives = [at_me([sent[p, j] if j > p else sent[last - p, last - j] for p in devices]) for j in devices]
    leaves = [at_me([summed[p, j] if j > p else summed[last - p, last - j] for p in devices]) for j in devices]
    far_leaves = [
        at_me([far.get((p, j) if j < middle else (last - p, last - j), -chunks) for p in devices]) for j in devices
    ]
    right_ends = at_me([summed[p, p] for p in devices])
    left_ends = at_me([summed[last - p, last - p] for p in devices])
    finish = jnp.maximum(right_ends, left_ends)
    slots = max(max(table.values()) for table in (sent, summed, far)) + chunks

    @pl.loop(0, slots)
    def _(slot):
        c_left = slot - own_left
        c_right = slot - own_right

        @pl.when(has_left & (c_left >= 0) & (c_left < chunks))
        def _():
            own_copy(c_left).start()

        @pl.when(has_right & (c_right >= 0) & (c_right < chunks))
        def _():
            block_copy(me, c_right, to_right).start()

        full_right = jnp.where(slot == 0, me, -1)
        full_left = jnp.int32(-1)
        for j in range(n_tp):
            c = slot - arrives[j]
            full = c == chunks - 1
            if j > 0:
                full_right = jnp.where(full & (j > me), j, full_right)

                @pl.when((j > me) & (c >= 0) & (c < chunks))
                def _():
                    block_copy(j, c, here).wait_recv()

                    @pl.when(has_left)
                    def _():
                        block_copy(j, c, to_left).start()

                    if j >= middle:

                        @pl.when(is_edge & jnp.logical_not(has_left))
                        def _():
                            far_weights_copy(j, c).start()

            if j < last:
                full_left = jnp.where(full & (j < me), j, full_left)

                @pl.when((j < me) & (c >= 0) & (c < chunks))
                def _():
                    block_copy(j, c, here).wait_recv()

                    @pl.when(has_right)
                    def _():
                        block_copy(j, c, to_right).start()

                    if j < middle:

                        @pl.when(is_edge & jnp.logical_not(has_right))
                        def _():
                            far_weights_copy(j, c).start()

        @pl.when((full_right >= 0) | (full_left >= 0))
        def _():
            @pl.loop(0, 2)
            def _(side):
                j = jnp.where(side == 0, full_right, full_left)

                @pl.when(j >= 0)
                def _():
                    compute(j)

        for j in range(n_tp):
            c = slot - leaves[j]
            if j > 0:

                @pl.when((j > me) & (c >= 0) & (c < chunks))
                def _():
                    @pl.when(has_left)
                    def _():
                        rightward(j, c, here).wait_recv()
                        from_left[j, c] = (from_left[j, c].astype(jnp.float32) + partials[j, c]).astype(jnp.bfloat16)

                    @pl.when(jnp.logical_not(has_left))
                    def _():
                        from_left[j, c] = partials[j, c].astype(jnp.bfloat16)

                    rightward(j, c, to_right).start()

            if j < last:

                @pl.when((j < me) & (c >= 0) & (c < chunks))
                def _():
                    @pl.when(has_right)
                    def _():
                        leftward(j, c, here).wait_recv()
                        from_right[j, c] = (from_right[j, c].astype(jnp.float32) + partials[j, c]).astype(
                            jnp.bfloat16
                        )

                    @pl.when(jnp.logical_not(has_right))
                    def _():
                        from_right[j, c] = partials[j, c].astype(jnp.bfloat16)

                    leftward(j, c, to_left).start()

        part = slot - right_ends
        piece = slot - left_ends

        @pl.when(has_left & (part >= 0) & (part < chunks))
        def _():
            rightward(me, part, here).wait_recv()

        @pl.when(has_right & (piece >= 0) & (piece < chunks))
        def _():
            leftward(me, piece, here).wait_recv()

        @pl.when(is_edge)
        def _():
            for j in range(n_tp):
                at = slot - far_leaves[j]
                goes_right = j < middle
                below = j <= me if goes_right else j >= me
                end = last if goes_right else 0

                @pl.when(below & (at >= 0) & (at < chunks))
                def _():
                    @pl.when(me == j)
                    def _():
                        begun = tracker[at].astype(jnp.float32) + partials[j, at]
                        if 0 < j < last:
                            begun = begun + (from_left if goes_right else from_right)[j, at].astype(jnp.float32)
                        to_far[j, at] = begun.astype(jnp.bfloat16)

                    @pl.when(me != j)
                    def _():
                        far_copy(j, at, here).wait_recv()
                        to_far[j, at] = (to_far[j, at].astype(jnp.float32) + partials[j, at]).astype(jnp.bfloat16)

                    @pl.when(me == end)
                    def _():
                        last_far_copy(j, at).start()

                    @pl.when(me != end)
                    def _():
                        far_copy(j, at, to_right if goes_right else to_left).start()

        done = slot - finish

        @pl.when((done >= 0) & (done < chunks))
        def _():
            @pl.when(has_left)
            def _():
                partials[me, done] = partials[me, done] + from_left[me, done].astype(jnp.float32)

            @pl.when(has_right)
            def _():
                partials[me, done] = partials[me, done] + from_right[me, done].astype(jnp.float32)

            rounded = partials[me, done].astype(jnp.bfloat16)
            gradient[done] = rounded
            outgoing[done] = (tracker[done].astype(jnp.float32) + rounded.astype(jnp.float32)).astype(jnp.bfloat16)
            for k in (0, 1, 2, 3):

                @pl.when(near[k])
                def _():
                    tracked_copy(k, done, torus[k]).start()

    for k in range(4):

        @pl.when(near[k])
        def _():
            mix_copy(k ^ 1, here).wait_recv()

    @pl.when(is_edge)
    def _():
        @pl.loop(0, chunks)
        def _(c):
            landed = near_weights.at[far_side, c]
            send(landed, landed, far_send.at[0, c], far_weights_recv.at[c], here).wait_recv()

    @pl.loop(0, chunks)
    def _(c):
        for k in range(4):
            tracked_copy(k ^ 1, c, here).wait_recv()
        own_gradient = gradient[c].astype(jnp.float32)
        tracked = tracker[c].astype(jnp.float32) + own_gradient
        weight_sum = blocks[me, c].astype(jnp.float32)
        tracked_sum = tracked
        for k in range(4):
            weight_sum = weight_sum + near_weights[k, c].astype(jnp.float32)
            tracked_sum = tracked_sum + near_tracked[k, c].astype(jnp.float32)
        new_weights_ref[c] = (weight_sum * 0.2 - learning_rate * tracked).astype(jnp.bfloat16)
        new_tracker_ref[c] = (tracked_sum * 0.2 - own_gradient).astype(jnp.bfloat16)

    for k in range(4):

        @pl.when(near[k])
        def _():
            mix_copy(k, torus[k]).wait_send()

    @pl.loop(0, chunks)
    def _(c):
        for k in range(4):

            @pl.when(near[k])
            def _():
                tracked_copy(k, c, torus[k]).wait_send()

        @pl.when(has_left)
        def _():
            own_copy(c).wait_send()

        @pl.when(has_right)
        def _():
            block_copy(me, c, here).wait_send()

        @pl.loop(0, n_tp)
        def _(j):
            passed = ((j > me) & has_left) | ((j < me) & has_right)
            farther = ((j >= middle) & (me == 0)) | ((j < middle) & (me == last))

            @pl.when(passed | (is_edge & farther))
            def _():
                block_copy(j, c, here).wait_send()

            @pl.when(is_edge & (((j < middle) & (j <= me)) | ((j >= middle) & (j >= me))))
            def _():
                far_copy(j, c, here).wait_send()

            @pl.when(j > me)
            def _():
                rightward(j, c, here).wait_send()

            @pl.when(j < me)
            def _():
                leftward(j, c, here).wait_send()


def on_device(sizes, weights, tracker, acts, cotangent):
    _, _, matrices, part_rows, model_width = weights.shape
    n_tp = sizes[2]
    used = matrices * part_rows
    rows = -(-used // 16) * 16
    width = model_width // chunks
    token_rows = acts.shape[2]

    def packed(values):
        flat = values.reshape(used, chunks, width)
        flat = jnp.pad(flat, ((0, rows - used), (0, 0), (0, 0)))
        return flat.transpose(1, 0, 2)

    def unpacked(values):
        return values.transpose(1, 0, 2)[:used].reshape(weights.shape)

    scales = (model_width ** (-0.5), (part_rows * n_tp) ** (-0.5))
    shape = (chunks, rows, width)
    half = jnp.bfloat16
    dma = pltpu.SemaphoreType.DMA
    new_weights, new_tracker = pl.pallas_call(
        functools.partial(kernel, sizes, scales, part_rows),
        out_shape=[jax.ShapeDtypeStruct(shape, half)] * 2,
        in_specs=[pl.BlockSpec(memory_space=pl.ANY)] * 4,
        out_specs=[pl.BlockSpec(memory_space=pltpu.VMEM)] * 2,
        scratch_shapes=[
            pltpu.VMEM((2 * token_rows, model_width), half),
            pltpu.VMEM((n_tp, *shape), half),
            pltpu.VMEM((n_tp, *shape), jnp.float32),
            pltpu.VMEM((n_tp, *shape), half),
            pltpu.VMEM((n_tp, *shape), half),
            pltpu.VMEM((n_tp, *shape), half),
            pltpu.VMEM(shape, half),
            pltpu.VMEM(shape, half),
            pltpu.VMEM(shape, half),
            pltpu.VMEM((4, *shape), half),
            pltpu.VMEM((4, *shape), half),
            dma((4,)),
            dma((n_tp, chunks)),
            dma((n_tp, chunks)),
            dma((chunks,)),
            dma((n_tp, chunks)),
            dma((n_tp, chunks)),
            dma((n_tp, chunks)),
            dma((n_tp, chunks)),
            dma((4,)),
            dma((4,)),
            dma((4, chunks)),
            dma((4, chunks)),
            dma((chunks,)),
            dma((n_tp, chunks)),
            dma((n_tp, chunks)),
        ],
        compiler_params=pltpu.CompilerParams(
            collective_id=0, has_side_effects=True, vmem_limit_bytes=48 * 1024 * 1024
        ),
        cost_estimate=pl.CostEstimate(flops=2_000_000_000, bytes_accessed=8_000_000, transcendentals=100_000),
    )(acts[0, 0], cotangent[0, 0], packed(weights), packed(tracker))
    return unpacked(new_weights), unpacked(new_tracker)


def solution(mesh):
    sizes = tuple(mesh.shape[axis] for axis in ("rx", "ry", "tp"))
    rows_split = P("rx", "ry", None, "tp", None)
    tokens_split = P("rx", "ry", "tp", None)
    return jax.shard_map(
        functools.partial(on_device, sizes),
        mesh=mesh,
        in_specs=(rows_split, rows_split, tokens_split, tokens_split),
        out_specs=(rows_split, rows_split),
        check_vma=False,
    )
```

```python
import functools

import jax
import jax.numpy as jnp
from jax import lax
from jax.experimental import pallas as pl
from jax.experimental.pallas import tpu as pltpu
from jax.sharding import PartitionSpec as P

MESH = pl.DeviceIdType.MESH

learning_rate = 0.1
chunks = 8
hop_slots = 5
compute_slots = 2
arrival_order = (1, 2, 3, 7, 6, 5, 4)


def timetable(n_tp):
    last = n_tp - 1
    sent, arrived, summed, far = {}, {}, {}, {}
    for p in range(last, -1, -1):
        free = 0
        for j in arrival_order + (0,):
            if j < p:
                continue
            slot = max(free, 0 if j == p else sent[p + 1, j] + hop_slots)
            if p == 0 and j > 0:
                slot = sent[1, j] + hop_slots
            sent[p, j] = slot
            free = slot + chunks
    for p in range(n_tp):
        free = 0
        for j in arrival_order:
            if j <= p:
                continue
            slot = max(free, sent[p, j] + chunks - 1 + compute_slots)
            if p > 0:
                slot = max(slot, summed[p - 1, j] + hop_slots)
            summed[p, j] = slot
            free = slot + chunks
    for j in range(n_tp):
        summed[j, j] = summed[j - 1, j] + hop_slots if j else 0
    for j in range(n_tp // 2):
        far[j, j] = summed[j, j]
        for p in range(j + 1, n_tp):
            far[p, j] = max(far[p - 1, j] + hop_slots, sent[last - p, last - j] + chunks - 1 + compute_slots)
    return sent, summed, far


def kernel(
    sizes,
    scales,
    part_rows,
    acts_hbm,
    cotangent_hbm,
    weights_hbm,
    tracker_hbm,
    new_weights_ref,
    new_tracker_ref,
    tokens,
    blocks,
    partials,
    from_left,
    from_right,
    to_far,
    tracker,
    gradient,
    outgoing,
    near_weights,
    near_tracked,
    load_sem,
    block_recv,
    block_send,
    own_send,
    left_recv,
    left_send,
    right_recv,
    right_send,
    mix_recv,
    mix_send,
    tracked_recv,
    tracked_send,
    far_weights_recv,
    far_recv,
    far_send,
):
    n_rx, n_ry, n_tp = sizes
    input_scale, output_scale = scales
    rx = lax.axis_index("rx")
    ry = lax.axis_index("ry")
    me = lax.axis_index("tp")
    last = n_tp - 1
    has_left = me > 0
    has_right = me < last
    torus = (
        (lax.rem(rx + 1, n_rx), ry, me),
        (lax.rem(rx + n_rx - 1, n_rx), ry, me),
        (rx, lax.rem(ry + 1, n_ry), me),
        (rx, lax.rem(ry + n_ry - 1, n_ry), me),
    )
    to_left = (rx, ry, me - 1)
    to_right = (rx, ry, me + 1)
    here = (rx, ry, me)

    place = lax.rem(rx, n_rx // 2)
    is_first = place == 0
    is_last = place == n_rx // 2 - 1
    is_edge = is_first | is_last
    near = (jnp.logical_not(is_last), jnp.logical_not(is_first), rx >= 0, rx >= 0)
    far_rx = jnp.where(is_last, torus[0][0], torus[1][0])
    far_side = jnp.where(is_last, 0, 1)
    middle = n_tp // 2
    feeder = (far_rx, ry, jnp.where(me < middle, last, 0))

    barrier = pltpu.get_barrier_semaphore()
    for exists, partner in zip(near, torus):

        @pl.when(exists)
        def _():
            pl.semaphore_signal(barrier, inc=1, device_id=partner, device_id_type=MESH)

    @pl.when(is_edge)
    def _():
        pl.semaphore_signal(barrier, inc=1, device_id=feeder, device_id_type=MESH)

    @pl.when(has_left)
    def _():
        pl.semaphore_signal(barrier, inc=1, device_id=to_left, device_id_type=MESH)

    @pl.when(has_right)
    def _():
        pl.semaphore_signal(barrier, inc=1, device_id=to_right, device_id_type=MESH)

    token_rows = acts_hbm.shape[0]
    loads = (
        pltpu.make_async_copy(weights_hbm, blocks.at[me], load_sem.at[0]),
        pltpu.make_async_copy(acts_hbm, tokens.at[pl.ds(0, token_rows)], load_sem.at[1]),
        pltpu.make_async_copy(cotangent_hbm, tokens.at[pl.ds(token_rows, token_rows)], load_sem.at[2]),
        pltpu.make_async_copy(tracker_hbm, tracker, load_sem.at[3]),
    )
    for load in loads:
        load.start()

    def send(source, target, send_sem, recv_sem, device):
        return pltpu.make_async_remote_copy(
            src_ref=source,
            dst_ref=target,
            send_sem=send_sem,
            recv_sem=recv_sem,
            device_id=device,
            device_id_type=MESH,
        )

    def block_copy(j, c, device):
        block = blocks.at[j, c]
        return send(block, block, block_send.at[j, c], block_recv.at[j, c], device)

    def own_copy(c):
        block = blocks.at[me, c]
        return send(block, block, own_send.at[c], block_recv.at[me, c], to_left)

    def rightward(j, c, device):
        block = from_left.at[j, c]
        return send(block, block, left_send.at[j, c], left_recv.at[j, c], device)

    def leftward(j, c, device):
        block = from_right.at[j, c]
        return send(block, block, right_send.at[j, c], right_recv.at[j, c], device)

    def mix_copy(k, device):
        return send(blocks.at[me], near_weights.at[k ^ 1], mix_send.at[k], mix_recv.at[k ^ 1], device)

    def tracked_copy(k, c, device):
        return send(
            outgoing.at[c], near_tracked.at[k ^ 1, c], tracked_send.at[k, c], tracked_recv.at[k ^ 1, c], device
        )

    def far_weights_copy(j, c):
        return send(
            blocks.at[j, c],
            near_weights.at[1 - far_side, c],
            block_send.at[j, c],
            far_weights_recv.at[c],
            (far_rx, ry, j),
        )

    def far_copy(j, c, device):
        block = to_far.at[j, c]
        return send(block, block, far_send.at[j, c], far_recv.at[j, c], device)

    def last_far_copy(j, c):
        return send(
            to_far.at[j, c],
            near_tracked.at[1 - far_side, c],
            far_send.at[j, c],
            tracked_recv.at[1 - far_side, c],
            (far_rx, ry, j),
        )

    loads[0].wait()
    expected = (
        jnp.where(is_edge, 3, 4)
        + jnp.where(has_left, 1, 0)
        + jnp.where(has_right, 1, 0)
        + jnp.where(is_edge & (me == 0), n_tp - middle, 0)
        + jnp.where(is_edge & (me == last), middle, 0)
    )
    pl.semaphore_wait(barrier, expected)

    for k in (2, 3, 0, 1):

        @pl.when(near[k])
        def _():
            mix_copy(k, torus[k]).start()

    for load in loads[1:]:
        load.wait()

    width = blocks.shape[3]
    rows = blocks.shape[2]
    row = lax.broadcasted_iota(jnp.int32, (rows, token_rows), 0)
    is_gate = row < part_rows
    is_up = (row >= part_rows) & (row < 2 * part_rows)
    is_down = (row >= 2 * part_rows) & (row < 3 * part_rows)
    row_scale = jnp.where(
        lax.broadcasted_iota(jnp.int32, (rows, 1), 0) < 2 * part_rows, input_scale, output_scale
    ).astype(jnp.float32)

    def compute(j):
        pre = jnp.zeros((rows, 2 * token_rows), jnp.float32)
        for c in range(chunks):
            pre += lax.dot_general(
                blocks[j, c],
                tokens[:, c * width : (c + 1) * width],
                (((1,), (1,)), ((), ())),
                preferred_element_type=jnp.float32,
            )
        gate = pre[:, :token_rows] * input_scale
        up = pltpu.roll(pre[:, :token_rows], rows - part_rows, 0) * input_scale
        hidden_grad = pltpu.roll(pre[:, token_rows:], rows - 2 * part_rows, 0) * output_scale
        sigmoid_gate = jax.nn.sigmoid(gate)
        gated = gate * sigmoid_gate
        hidden = gated * up
        up_grad = hidden_grad * gated
        gate_grad = hidden_grad * up * sigmoid_gate * (1.0 + gate * (1.0 - sigmoid_gate))
        with_tokens = jnp.where(is_gate, gate_grad, jnp.where(is_up, pltpu.roll(up_grad, part_rows, 0), 0.0))
        with_cotangent = jnp.where(is_down, pltpu.roll(hidden, 2 * part_rows, 0), 0.0)
        both = jnp.concatenate([with_tokens, with_cotangent], axis=1).astype(jnp.bfloat16)
        for c in range(chunks):
            partials[j, c] = (
                jnp.dot(both, tokens[:, c * width : (c + 1) * width], preferred_element_type=jnp.float32) * row_scale
            )

    sent, summed, far = timetable(n_tp)

    def at_me(values):
        chosen = jnp.int32(values[0])
        for p in range(1, n_tp):
            chosen = jnp.where(me == p, values[p], chosen)
        return chosen

    devices = range(n_tp)
    own_left = at_me([sent[p, p] for p in devices])
    own_right = at_me([sent[last - p, last - p] for p in devices])
    arrives = [at_me([sent[p, j] if j > p else sent[last - p, last - j] for p in devices]) for j in devices]
    leaves = [at_me([summed[p, j] if j > p else summed[last - p, last - j] for p in devices]) for j in devices]
    far_leaves = [
        at_me([far.get((p, j) if j < middle else (last - p, last - j), -chunks) for p in devices]) for j in devices
    ]
    right_ends = at_me([summed[p, p] for p in devices])
    left_ends = at_me([summed[last - p, last - p] for p in devices])
    finish = jnp.maximum(right_ends, left_ends)
    slots = max(max(table.values()) for table in (sent, summed, far)) + chunks

    @pl.loop(0, slots)
    def _(slot):
        c_left = slot - own_left
        c_right = slot - own_right

        @pl.when(has_left & (c_left >= 0) & (c_left < chunks))
        def _():
            own_copy(c_left).start()

        @pl.when(has_right & (c_right >= 0) & (c_right < chunks))
        def _():
            block_copy(me, c_right, to_right).start()

        full_right = jnp.where(slot == 0, me, -1)
        full_left = jnp.int32(-1)
        for j in range(n_tp):
            c = slot - arrives[j]
            full = c == chunks - 1
            if j > 0:
                full_right = jnp.where(full & (j > me), j, full_right)

                @pl.when((j > me) & (c >= 0) & (c < chunks))
                def _():
                    block_copy(j, c, here).wait_recv()

                    @pl.when(has_left)
                    def _():
                        block_copy(j, c, to_left).start()

                    if j >= middle:

                        @pl.when(is_edge & jnp.logical_not(has_left))
                        def _():
                            far_weights_copy(j, c).start()

            if j < last:
                full_left = jnp.where(full & (j < me), j, full_left)

                @pl.when((j < me) & (c >= 0) & (c < chunks))
                def _():
                    block_copy(j, c, here).wait_recv()

                    @pl.when(has_right)
                    def _():
                        block_copy(j, c, to_right).start()

                    if j < middle:

                        @pl.when(is_edge & jnp.logical_not(has_right))
                        def _():
                            far_weights_copy(j, c).start()

        @pl.when((full_right >= 0) | (full_left >= 0))
        def _():
            @pl.loop(0, 2)
            def _(side):
                j = jnp.where(side == 0, full_right, full_left)

                @pl.when(j >= 0)
                def _():
                    compute(j)

        for j in range(n_tp):
            c = slot - leaves[j]
            if j > 0:

                @pl.when((j > me) & (c >= 0) & (c < chunks))
                def _():
                    @pl.when(has_left)
                    def _():
                        rightward(j, c, here).wait_recv()
                        from_left[j, c] = (from_left[j, c].astype(jnp.float32) + partials[j, c]).astype(jnp.bfloat16)

                    @pl.when(jnp.logical_not(has_left))
                    def _():
                        from_left[j, c] = partials[j, c].astype(jnp.bfloat16)

                    rightward(j, c, to_right).start()

            if j < last:

                @pl.when((j < me) & (c >= 0) & (c < chunks))
                def _():
                    @pl.when(has_right)
                    def _():
                        leftward(j, c, here).wait_recv()
                        from_right[j, c] = (from_right[j, c].astype(jnp.float32) + partials[j, c]).astype(
                            jnp.bfloat16
                        )

                    @pl.when(jnp.logical_not(has_right))
                    def _():
                        from_right[j, c] = partials[j, c].astype(jnp.bfloat16)

                    leftward(j, c, to_left).start()

        part = slot - right_ends
        piece = slot - left_ends

        @pl.when(has_left & (part >= 0) & (part < chunks))
        def _():
            rightward(me, part, here).wait_recv()

        @pl.when(has_right & (piece >= 0) & (piece < chunks))
        def _():
            leftward(me, piece, here).wait_recv()

        @pl.when(is_edge)
        def _():
            for j in range(n_tp):
                at = slot - far_leaves[j]
                goes_right = j < middle
                below = j <= me if goes_right else j >= me
                end = last if goes_right else 0

                @pl.when(below & (at >= 0) & (at < chunks))
                def _():
                    @pl.when(me == j)
                    def _():
                        begun = tracker[at].astype(jnp.float32) + partials[j, at]
                        if 0 < j < last:
                            begun = begun + (from_left if goes_right else from_right)[j, at].astype(jnp.float32)
                        to_far[j, at] = begun.astype(jnp.bfloat16)

                    @pl.when(me != j)
                    def _():
                        far_copy(j, at, here).wait_recv()
                        to_far[j, at] = (to_far[j, at].astype(jnp.float32) + partials[j, at]).astype(jnp.bfloat16)

                    @pl.when(me == end)
                    def _():
                        last_far_copy(j, at).start()

                    @pl.when(me != end)
                    def _():
                        far_copy(j, at, to_right if goes_right else to_left).start()

        done = slot - finish

        @pl.when((done >= 0) & (done < chunks))
        def _():
            @pl.when(has_left)
            def _():
                partials[me, done] = partials[me, done] + from_left[me, done].astype(jnp.float32)

            @pl.when(has_right)
            def _():
                partials[me, done] = partials[me, done] + from_right[me, done].astype(jnp.float32)

            rounded = partials[me, done].astype(jnp.bfloat16)
            gradient[done] = rounded
            outgoing[done] = (tracker[done].astype(jnp.float32) + rounded.astype(jnp.float32)).astype(jnp.bfloat16)
            for k in (0, 1, 2, 3):

                @pl.when(near[k])
                def _():
                    tracked_copy(k, done, torus[k]).start()

    for k in range(4):

        @pl.when(near[k])
        def _():
            mix_copy(k ^ 1, here).wait_recv()

    @pl.when(is_edge)
    def _():
        @pl.loop(0, chunks)
        def _(c):
            landed = near_weights.at[far_side, c]
            send(landed, landed, far_send.at[0, c], far_weights_recv.at[c], here).wait_recv()

    @pl.loop(0, chunks)
    def _(c):
        for k in range(4):
            tracked_copy(k ^ 1, c, here).wait_recv()
        own_gradient = gradient[c].astype(jnp.float32)
        tracked = tracker[c].astype(jnp.float32) + own_gradient
        weight_sum = blocks[me, c].astype(jnp.float32)
        tracked_sum = tracked
        for k in range(4):
            weight_sum = weight_sum + near_weights[k, c].astype(jnp.float32)
            tracked_sum = tracked_sum + near_tracked[k, c].astype(jnp.float32)
        new_weights_ref[c] = (weight_sum * 0.2 - learning_rate * tracked).astype(jnp.bfloat16)
        new_tracker_ref[c] = (tracked_sum * 0.2 - own_gradient).astype(jnp.bfloat16)

    for k in range(4):

        @pl.when(near[k])
        def _():
            mix_copy(k, torus[k]).wait_send()

    @pl.loop(0, chunks)
    def _(c):
        for k in range(4):

            @pl.when(near[k])
            def _():
                tracked_copy(k, c, torus[k]).wait_send()

        @pl.when(has_left)
        def _():
            own_copy(c).wait_send()

        @pl.when(has_right)
        def _():
            block_copy(me, c, here).wait_send()

        @pl.loop(0, n_tp)
        def _(j):
            passed = ((j > me) & has_left) | ((j < me) & has_right)
            farther = ((j >= middle) & (me == 0)) | ((j < middle) & (me == last))

            @pl.when(passed | (is_edge & farther))
            def _():
                block_copy(j, c, here).wait_send()

            @pl.when(is_edge & (((j < middle) & (j <= me)) | ((j >= middle) & (j >= me))))
            def _():
                far_copy(j, c, here).wait_send()

            @pl.when(j > me)
            def _():
                rightward(j, c, here).wait_send()

            @pl.when(j < me)
            def _():
                leftward(j, c, here).wait_send()


def on_device(sizes, weights, tracker, acts, cotangent):
    _, _, matrices, part_rows, model_width = weights.shape
    n_tp = sizes[2]
    used = matrices * part_rows
    rows = -(-used // 16) * 16
    width = model_width // chunks
    token_rows = acts.shape[2]

    def packed(values):
        flat = values.reshape(used, chunks, width)
        flat = jnp.pad(flat, ((0, rows - used), (0, 0), (0, 0)))
        return flat.transpose(1, 0, 2)

    def unpacked(values):
        return values.transpose(1, 0, 2)[:used].reshape(weights.shape)

    scales = (model_width ** (-0.5), (part_rows * n_tp) ** (-0.5))
    shape = (chunks, rows, width)
    half = jnp.bfloat16
    dma = pltpu.SemaphoreType.DMA
    new_weights, new_tracker = pl.pallas_call(
        functools.partial(kernel, sizes, scales, part_rows),
        out_shape=[jax.ShapeDtypeStruct(shape, half)] * 2,
        in_specs=[pl.BlockSpec(memory_space=pl.ANY)] * 4,
        out_specs=[pl.BlockSpec(memory_space=pltpu.VMEM)] * 2,
        scratch_shapes=[
            pltpu.VMEM((2 * token_rows, model_width), half),
            pltpu.VMEM((n_tp, *shape), half),
            pltpu.VMEM((n_tp, *shape), jnp.float32),
            pltpu.VMEM((n_tp, *shape), half),
            pltpu.VMEM((n_tp, *shape), half),
            pltpu.VMEM((n_tp, *shape), half),
            pltpu.VMEM(shape, half),
            pltpu.VMEM(shape, half),
            pltpu.VMEM(shape, half),
            pltpu.VMEM((4, *shape), half),
            pltpu.VMEM((4, *shape), half),
            dma((4,)),
            dma((n_tp, chunks)),
            dma((n_tp, chunks)),
            dma((chunks,)),
            dma((n_tp, chunks)),
            dma((n_tp, chunks)),
            dma((n_tp, chunks)),
            dma((n_tp, chunks)),
            dma((4,)),
            dma((4,)),
            dma((4, chunks)),
            dma((4, chunks)),
            dma((chunks,)),
            dma((n_tp, chunks)),
            dma((n_tp, chunks)),
        ],
        compiler_params=pltpu.CompilerParams(
            collective_id=0, has_side_effects=True, vmem_limit_bytes=48 * 1024 * 1024
        ),
        cost_estimate=pl.CostEstimate(flops=2_000_000_000, bytes_accessed=8_000_000, transcendentals=100_000),
    )(acts[0, 0], cotangent[0, 0], packed(weights), packed(tracker))
    return unpacked(new_weights), unpacked(new_tracker)


def solution(mesh):
    sizes = tuple(mesh.shape[axis] for axis in ("rx", "ry", "tp"))
    rows_split = P("rx", "ry", None, "tp", None)
    tokens_split = P("rx", "ry", "tp", None)
    return jax.shard_map(
        functools.partial(on_device, sizes),
        mesh=mesh,
        in_specs=(rows_split, rows_split, tokens_split, tokens_split),
        out_specs=(rows_split, rows_split),
        check_vma=False,
    )
```
